512 devices in a mesh: expert: 16 (over x, z_lo), shard: 32 (over z_hi, y, core).
Axes of the slice: x: 4, y: 4, z: 16 (z_hi: 4, z_lo: 4; z = z_hi * 4 + z_lo), core: 2. Of those that a mesh axis runs over, the one named last changes fastest.
Arguments:
- tokens: bfloat16 [65536, 3072], P(('expert', 'shard')), may hold values from -6 to 6
- expert_ids: int32 [65536, 1], P(('expert', 'shard')), may hold values from 0 to 63, as said below
- gate_weight: bfloat16 [64, 1024, 3072], P('expert', 'shard'), may hold values from -0.109375 to 0.109375
- up_weight: bfloat16 [64, 1024, 3072], P('expert', 'shard'), may hold values from -0.109375 to 0.109375
- down_weight: bfloat16 [64, 1024, 3072], P('expert', 'shard'), may hold values from -0.1875 to 0.1875
Outputs:
- moe_output: bfloat16 [65536, 3072], P(('expert', 'shard'))
The draws below stay inside these ranges and needn't reach their ends.
Inputs may be any that keep to these rules, and one draw needn't show every extreme that they name: `expert_ids`: among each device's 128 tokens no expert is named more than 3 times; one expert, the same on every device, is named exactly 3 times on every device.
All inputs are finite; a program needn't handle non-finite values.
Results may differ from the reference program's by a relative error of at most 0.0049.
Values may be sent and summed in bfloat16 or wider, within the bound.
No kernel may reach another device: no remote copies, remote signals or barrier semaphores. Data moves between devices by JAX's collectives and lax.ppermute only.
A program may use at most 64 MiB of HBM per device.

```python
import jax
import jax.numpy as jnp
from jax import lax

D = 3072
FF = 1024
TOK_DEV = 128
EXPERTS = 64
TOKENS = 65536
CAP = 3
SLOTS = 1536


def draw_expert_ids(key, part):
    others = EXPERTS - 1
    key_hot, key_rank, key_rows = jax.random.split(key, 3)
    hot_expert = jax.random.randint(key_hot, (), 0, EXPERTS).astype(jnp.int32)
    rank_order = jax.random.permutation(key_rank, jnp.arange(others, dtype=jnp.int32))
    preference = (1024 // (1 + rank_order)).astype(jnp.int32)
    item_index = jnp.arange(others * CAP, dtype=jnp.int32).reshape(others, CAP)

    def one_block(block_key):
        key_score, key_perm = jax.random.split(block_key)
        base_score = jax.random.randint(key_score, (others, CAP), 0, 1024).astype(jnp.int32)
        scores = (base_score + preference[:, None]) * 8192 + item_index
        _, picked = lax.top_k(scores.reshape(-1), TOK_DEV - CAP)
        chosen = (picked // CAP).astype(jnp.int32)
        chosen = chosen + (chosen >= hot_expert).astype(jnp.int32)
        block_ids = jnp.concatenate([jnp.zeros((CAP,), jnp.int32) + hot_expert, chosen])
        return jax.random.permutation(key_perm, block_ids)
    block_keys = jax.random.split(key_rows, TOKENS // TOK_DEV)
    return jax.vmap(one_block)(block_keys).reshape(TOKENS, 1).astype(jnp.int32)


def steps_of(stream_key, dims, cuts, least, top_value):
    factor_of = 1.0
    for dim, shards_of in cuts:
        heights = jax.random.uniform(jax.random.fold_in(jax.random.fold_in(stream_key, 6), dim), (shards_of,), jnp.float32, least / len(cuts), top_value / len(cuts))
        factor_of = factor_of * jnp.repeat(jnp.exp(heights), dims[dim] // shards_of).reshape((-1,) + (1,) * (len(dims) - 1 - dim))
    return factor_of


def normal_values(key, extent, deviation, limit, shards=(), held_as=jnp.bfloat16):
    values = jax.random.normal(key, extent, jnp.float32) * deviation
    if len(shards) > 0:
        values = steps_of(key, extent, shards, -0.22, 0.18) * values
    return jnp.clip(values, min=-limit, max=limit).astype(held_as)


def setup_inputs(seed: int = 0) -> dict:
    splits = jax.random.split(jax.random.key(seed), 6)
    return {
        "tokens": normal_values(splits[0], (TOKENS, D), 1.0, 6.0, ((0, 512),)),
        "expert_ids": draw_expert_ids(jax.random.fold_in(splits[5], 71), 0),
        "gate_weight": normal_values(splits[2], (EXPERTS, FF, D), D ** -0.5, 0.109375, ((0, 16), (1, 32))),
        "up_weight": normal_values(splits[3], (EXPERTS, FF, D), D ** -0.5, 0.109375, ((0, 16), (1, 32))),
        "down_weight": normal_values(splits[4], (EXPERTS, FF, D), FF ** -0.5, 0.1875, ((0, 16), (1, 32))),
    }


def expert_block(tokens, gate_mat, up_mat, down_mat, row_ids, is_valid):
    chosen = tokens[row_ids]
    gate_value = jnp.dot(chosen, gate_mat.T, preferred_element_type=jnp.float32)
    up_value = jnp.dot(chosen, up_mat.T, preferred_element_type=jnp.float32)
    hidden = (jax.nn.silu(gate_value) * up_value).astype(jnp.bfloat16)
    block_out = jnp.dot(hidden, down_mat, preferred_element_type=jnp.float32).astype(tokens.dtype)
    return jnp.where(is_valid[:, None], block_out, jnp.zeros_like(block_out))


def reference(tokens, expert_ids, gate_weight, up_weight, down_weight):
    flat_ids = expert_ids[:, 0].astype(jnp.int32)
    experts_all = gate_weight.shape[0]
    sorted_rows = jnp.argsort(flat_ids, stable=True).astype(jnp.int32)
    matches = (flat_ids[:, None] == jnp.arange(experts_all, dtype=jnp.int32)[None, :]).astype(jnp.int32)
    counts = jnp.sum(matches, axis=0).astype(jnp.int32)
    starts = (jnp.cumsum(counts) - counts).astype(jnp.int32)
    slot_bound = SLOTS
    padded = jnp.concatenate([sorted_rows, jnp.zeros((slot_bound,), jnp.int32)])

    def add_expert(result, expert_index):
        row_ids = lax.dynamic_slice(padded, (starts[expert_index],), (slot_bound,))
        is_valid = jnp.arange(slot_bound, dtype=jnp.int32) < counts[expert_index]
        block_out = expert_block(tokens, gate_weight[expert_index], up_weight[expert_index], down_weight[expert_index], row_ids, is_valid)
        return result.at[row_ids].add(block_out), None

    result, _ = lax.scan(add_expert, jnp.zeros(tokens.shape, tokens.dtype), jnp.arange(experts_all, dtype=jnp.int32))
    return result
```

```python
import jax
import jax.numpy as jnp
from jax import lax
from jax.sharding import Mesh, PartitionSpec as P

CAP = 3
CHUNKS = 8


def shards(tokens, expert_ids, gate_weight, up_weight, down_weight):
    exp_dev, unit_rows, width = gate_weight.shape
    rows = tokens.shape[0]
    routes = ("x", "zlo", "zhi")
    plane = ("y", "core")
    experts = exp_dev * lax.axis_size("x") * lax.axis_size("zlo")
    chunk = width // CHUNKS
    slots = experts * CAP

    def owned(weight):
        part = lax.all_to_all(weight, "zhi", split_axis=0, concat_axis=0, tiled=True)
        return lax.all_gather(part, plane, axis=0, tiled=True).reshape(-1, width)

    gate_full = owned(gate_weight)
    up_full = owned(up_weight)
    down_full = owned(down_weight)

    flat_ids = expert_ids[:, 0]
    matches = (flat_ids[:, None] == jnp.arange(experts, dtype=jnp.int32)[None, :]).astype(jnp.int32)
    rank_of = jnp.sum((jnp.cumsum(matches, axis=0) - 1) * matches, axis=1)
    position = flat_ids * CAP + rank_of
    selector = (position[None, :] == jnp.arange(slots, dtype=jnp.int32)[:, None]).astype(jnp.bfloat16)
    packed = jnp.dot(selector, tokens, preferred_element_type=jnp.float32).astype(jnp.bfloat16)
    packed = packed.reshape(experts, CAP * CHUNKS, chunk)
    arrived = lax.all_to_all(packed, routes, split_axis=0, concat_axis=0, tiled=True)
    arrived = arrived.reshape(slots, width)
    gate_value = lax.dot_general(
        arrived, gate_full, (((1,), (1,)), ((), ())), preferred_element_type=jnp.float32
    )
    up_value = lax.dot_general(
        arrived, up_full, (((1,), (1,)), ((), ())), preferred_element_type=jnp.float32
    )
    hidden = (jax.nn.silu(gate_value) * up_value).astype(jnp.bfloat16)
    result = jnp.dot(hidden, down_full, preferred_element_type=jnp.float32).astype(jnp.bfloat16)
    result = result.reshape(experts, CAP * CHUNKS, chunk)
    returned = lax.all_to_all(result, routes, split_axis=0, concat_axis=0, tiled=True)
    returned = returned.reshape(slots, width)
    output = lax.dot_general(
        selector, returned, (((0,), (0,)), ((), ())), preferred_element_type=jnp.float32
    )
    return output.astype(jnp.bfloat16)


def solution(mesh):
    fine = Mesh(mesh.devices.reshape(4, 4, 4, 4, 2), ("x", "zlo", "zhi", "y", "core"))
    everyone = ("x", "zlo", "zhi", "y", "core")
    group = ("x", "zlo")
    sub = ("zhi", "y", "core")
    return jax.shard_map(
        shards,
        mesh=fine,
        in_specs=(
            P(everyone, None),
            P(everyone, None),
            P(group, sub, None),
            P(group, sub, None),
            P(group, sub, None),
        ),
        out_specs=P(everyone, None),
        check_vma=False,
    )
```

```python
import jax
import jax.numpy as jnp
from jax import lax
from jax.sharding import Mesh, PartitionSpec as P

CAP = 3
CHUNKS = 8


def shards(tokens, expert_ids, gate_weight, up_weight, down_weight):
    exp_dev, unit_rows, width = gate_weight.shape
    rows = tokens.shape[0]
    routes = ("x", "zlo", "zhi")
    plane = ("y", "core")
    experts = exp_dev * lax.axis_size("x") * lax.axis_size("zlo")
    chunk = width // CHUNKS
    slots = experts * CAP

    ring = lax.axis_size("zhi")
    place = lax.axis_index("zhi")

    def piece(weight, step):
        return lax.dynamic_slice_in_dim(weight, lax.rem(place + step, ring), 1, 0)

    def passed(value, step):
        return lax.ppermute(value, "zhi", [(i, (i + step) % ring) for i in range(ring)])

    held = []
    previous = None
    for weight in (gate_weight, up_weight, down_weight):
        outgoing = [piece(weight, step) for step in range(ring)]
        if previous is not None:
            for step in range(1, ring):
                outgoing[step], previous[step] = lax.optimization_barrier(
                    (outgoing[step], previous[step])
                )
            held[-1] = previous
        previous = [outgoing[0]] + [passed(outgoing[step], step) for step in range(1, ring)]
        held.append(previous)
    own = [jnp.concatenate(pieces, axis=0) for pieces in held]
    tokens, own[2] = lax.optimization_barrier((tokens, own[2]))
    gate_full, up_full, down_full = (
        lax.all_gather(part, plane, axis=0, tiled=True).reshape(-1, width) for part in own
    )

    flat_ids = expert_ids[:, 0]
    matches = (flat_ids[:, None] == jnp.arange(experts, dtype=jnp.int32)[None, :]).astype(jnp.int32)
    rank_of = jnp.sum((jnp.cumsum(matches, axis=0) - 1) * matches, axis=1)
    position = flat_ids * CAP + rank_of
    selector = (position[None, :] == jnp.arange(slots, dtype=jnp.int32)[:, None]).astype(jnp.bfloat16)
    packed = jnp.dot(selector, tokens, preferred_element_type=jnp.float32).astype(jnp.bfloat16)
    packed = packed.reshape(experts, CAP * CHUNKS, chunk)
    arrived = lax.all_to_all(packed, routes, split_axis=0, concat_axis=0, tiled=True)
    arrived = arrived.reshape(slots, width)
    gate_value = lax.dot_general(
        arrived, gate_full, (((1,), (1,)), ((), ())), preferred_element_type=jnp.float32
    )
    up_value = lax.dot_general(
        arrived, up_full, (((1,), (1,)), ((), ())), preferred_element_type=jnp.float32
    )
    hidden = (jax.nn.silu(gate_value) * up_value).astype(jnp.bfloat16)
    hidden = lax.optimization_barrier(hidden)
    result = jnp.dot(hidden, down_full, preferred_element_type=jnp.float32).astype(jnp.bfloat16)
    result = result.reshape(experts, CAP * CHUNKS, chunk)
    returned = lax.all_to_all(result, routes, split_axis=0, concat_axis=0, tiled=True)
    returned = returned.reshape(slots, width)
    output = lax.dot_general(
        selector, returned, (((0,), (0,)), ((), ())), preferred_element_type=jnp.float32
    )
    return output.astype(jnp.bfloat16)


def solution(mesh):
    fine = Mesh(mesh.devices.reshape(4, 4, 4, 4, 2), ("x", "zlo", "zhi", "y", "core"))
    everyone = ("x", "zlo", "zhi", "y", "core")
    group = ("x", "zlo")
    sub = ("zhi", "y", "core")
    return jax.shard_map(
        shards,
        mesh=fine,
        in_specs=(
            P(everyone, None),
            P(everyone, None),
            P(group, sub, None),
            P(group, sub, None),
            P(group, sub, None),
        ),
        out_specs=P(everyone, None),
        check_vma=False,
    )
```

```python
import jax
import jax.numpy as jnp
from jax import lax
from jax.experimental import pallas as pl
from jax.experimental.pallas import tpu as pltpu
from jax.sharding import Mesh, PartitionSpec as P

CAP = 3
CHUNKS = 8
PARTS = 2
MIB = 1 << 20


def swiglu_kernel(x_ref, *refs):
    weights, (out_ref, held, total, arrival) = refs[:-4], refs[-4:]
    blocks, triple, width = weights[0].shape
    rows = triple // 3
    copies = [
        pltpu.make_async_copy(weight, held.at[i], arrival.at[i]) for i, weight in enumerate(weights)
    ]
    for copy in copies:
        copy.start()
    across = (((1,), (1,)), ((), ()))
    for i, copy in enumerate(copies):
        copy.wait()

        def matrix(which):
            return held[i, :, which * rows : (which + 1) * rows, :].reshape(blocks * rows, width)

        gate = lax.dot_general(x_ref[...], matrix(0), across, preferred_element_type=jnp.float32)
        up = lax.dot_general(x_ref[...], matrix(1), across, preferred_element_type=jnp.float32)
        hidden = (gate / (1.0 + jnp.exp(-gate)) * up).astype(jnp.bfloat16)
        product = jnp.dot(hidden, matrix(2), preferred_element_type=jnp.float32)
        if i == 0:
            total[...] = product
        elif i < len(copies) - 1:
            total[...] += product
        else:
            out_ref[...] = (total[...] + product).astype(out_ref.dtype)


def swiglu(x, weights):
    slots, width = x.shape
    blocks, triple, _ = weights[0].shape
    units = len(weights) * blocks * triple // 3
    return pl.pallas_call(
        swiglu_kernel,
        out_shape=jax.ShapeDtypeStruct(x.shape, jnp.bfloat16),
        in_specs=[pl.BlockSpec(memory_space=pltpu.VMEM)]
        + [pl.BlockSpec(memory_space=pl.ANY)] * len(weights),
        out_specs=pl.BlockSpec(memory_space=pltpu.VMEM),
        scratch_shapes=[
            pltpu.VMEM((len(weights), blocks, triple, width), jnp.bfloat16),
            pltpu.VMEM((slots, width), jnp.float32),
            pltpu.SemaphoreType.DMA((len(weights),)),
        ],
        compiler_params=pltpu.CompilerParams(vmem_limit_bytes=48 * MIB),
        cost_estimate=pl.CostEstimate(
            flops=6 * slots * units * width,
            bytes_accessed=6 * units * width + 4 * slots * width,
            transcendentals=slots * units,
        ),
    )(x, *weights)


def shards(tokens, expert_ids, gate_weight, up_weight, down_weight):
    exp_dev, unit_rows, width = gate_weight.shape
    routes = ("x", "zlo", "zhi")
    experts = exp_dev * lax.axis_size("x") * lax.axis_size("zlo")
    chunk = width // CHUNKS
    slots = experts * CAP
    ring = lax.axis_size("zhi")
    place = lax.axis_index("zhi")
    part_rows = unit_rows // PARTS

    def tied(*values):
        return lax.optimization_barrier(values)

    def shifted(value, axis, step):
        size = lax.axis_size(axis)
        return lax.ppermute(value, axis, [(i, (i + step) % size) for i in range(size)])

    def outgoing(step, part):
        target = lax.rem(place + step, ring)
        return jnp.concatenate(
            [
                lax.dynamic_slice(w, (target, part * part_rows, 0), (1, part_rows, width))
                for w in (gate_weight, up_weight, down_weight)
            ],
            axis=1,
        )

    def over_z(pieces):
        order = sorted(range(1, ring), key=lambda step: abs(2 * step - ring))
        return [shifted(pieces[step], "zhi", step) for step in order] + [pieces[0]]

    def over_plane(part):
        return lax.all_gather(part, ("y", "core"), axis=0, tiled=True)

    def joined(pieces):
        return jnp.concatenate(pieces, axis=0)

    early = tied(*[outgoing(step, 0) for step in range(ring)])
    late = tied(*[outgoing(step, 1) for step in range(ring)])
    first = joined(tied(*over_z(list(early))))
    first, *late = tied(first, *late)
    second = joined(tied(*over_z(late)))
    tokens, second = tied(tokens, second)
    first, second = over_plane(first), over_plane(second)

    flat_ids = expert_ids[:, 0]
    matches = (flat_ids[:, None] == jnp.arange(experts, dtype=jnp.int32)[None, :]).astype(jnp.int32)
    rank_of = jnp.sum((jnp.cumsum(matches, axis=0) - 1) * matches, axis=1)
    position = flat_ids * CAP + rank_of
    selector = (position[None, :] == jnp.arange(slots, dtype=jnp.int32)[:, None]).astype(jnp.bfloat16)
    packed = jnp.dot(selector, tokens, preferred_element_type=jnp.float32).astype(jnp.bfloat16)
    packed = packed.reshape(experts, CAP * CHUNKS, chunk)
    arrived = lax.all_to_all(packed, routes, split_axis=0, concat_axis=0, tiled=True)

    result = swiglu(arrived.reshape(slots, width), [first, second])
    result = result.reshape(experts, CAP * CHUNKS, chunk)
    returned = lax.all_to_all(result, routes, split_axis=0, concat_axis=0, tiled=True)
    returned = returned.reshape(slots, width)
    output = lax.dot_general(
        selector, returned, (((0,), (0,)), ((), ())), preferred_element_type=jnp.float32
    )
    return output.astype(jnp.bfloat16)


def solution(mesh):
    fine = Mesh(mesh.devices.reshape(4, 4, 4, 4, 2), ("x", "zlo", "zhi", "y", "core"))
    everyone = ("x", "zlo", "zhi", "y", "core")
    group = ("x", "zlo")
    sub = ("zhi", "y", "core")
    return jax.shard_map(
        shards,
        mesh=fine,
        in_specs=(
            P(everyone, None),
            P(everyone, None),
            P(group, sub, None),
            P(group, sub, None),
            P(group, sub, None),
        ),
        out_specs=P(everyone, None),
        check_vma=False,
    )
```

```python
import jax
import jax.numpy as jnp
from jax import lax
from jax.experimental import pallas as pl
from jax.experimental.pallas import tpu as pltpu
from jax.sharding import Mesh, PartitionSpec as P

CAP = 3
CHUNKS = 8
PARTS = 2
PIECES = 4
AHEAD = 2
MIB = 1 << 20


def swiglu_kernel(x_ref, *refs):
    weights, (out_ref, held, total, arrival) = refs[:-4], refs[-4:]
    pieces, blocks, triple, width = held.shape
    rows = triple // 3
    each = pieces // len(weights)
    copies = [
        pltpu.make_async_copy(
            weights[i // each].at[pl.ds(i % each * blocks, blocks)], held.at[i], arrival.at[i]
        )
        for i in range(pieces)
    ]
    for copy in copies[:AHEAD]:
        copy.start()
    across = (((1,), (1,)), ((), ()))
    for i, copy in enumerate(copies):
        copy.wait()
        for later in copies[i + AHEAD : i + AHEAD + 1]:
            later.start()

        def matrix(which):
            return held[i, :, which * rows : (which + 1) * rows, :].reshape(blocks * rows, width)

        gate = lax.dot_general(x_ref[...], matrix(0), across, preferred_element_type=jnp.float32)
        up = lax.dot_general(x_ref[...], matrix(1), across, preferred_element_type=jnp.float32)
        hidden = (gate / (1.0 + jnp.exp(-gate)) * up).astype(jnp.bfloat16)
        product = jnp.dot(hidden, matrix(2), preferred_element_type=jnp.float32)
        if i == 0:
            total[...] = product
        elif i < len(copies) - 1:
            total[...] += product
        else:
            out_ref[...] = (total[...] + product).astype(out_ref.dtype)


def swiglu(x, weights):
    slots, width = x.shape
    blocks, triple, _ = weights[0].shape
    units = len(weights) * blocks * triple // 3
    return pl.pallas_call(
        swiglu_kernel,
        out_shape=jax.ShapeDtypeStruct(x.shape, jnp.bfloat16),
        in_specs=[pl.BlockSpec(memory_space=pltpu.VMEM)]
        + [pl.BlockSpec(memory_space=pl.ANY)] * len(weights),
        out_specs=pl.BlockSpec(memory_space=pltpu.VMEM),
        scratch_shapes=[
            pltpu.VMEM((PIECES, len(weights) * blocks // PIECES, triple, width), jnp.bfloat16),
            pltpu.VMEM((slots, width), jnp.float32),
            pltpu.SemaphoreType.DMA((PIECES,)),
        ],
        compiler_params=pltpu.CompilerParams(vmem_limit_bytes=48 * MIB),
        cost_estimate=pl.CostEstimate(
            flops=6 * slots * units * width,
            bytes_accessed=6 * units * width + 4 * slots * width,
            transcendentals=slots * units,
        ),
    )(x, *weights)


def shards(tokens, expert_ids, gate_weight, up_weight, down_weight):
    exp_dev, unit_rows, width = gate_weight.shape
    routes = ("x", "zlo", "zhi")
    experts = exp_dev * lax.axis_size("x") * lax.axis_size("zlo")
    chunk = width // CHUNKS
    slots = experts * CAP
    ring = lax.axis_size("zhi")
    place = lax.axis_index("zhi")
    part_rows = unit_rows // PARTS

    def tied(*values):
        return lax.optimization_barrier(values)

    def shifted(value, axis, step):
        size = lax.axis_size(axis)
        return lax.ppermute(value, axis, [(i, (i + step) % size) for i in range(size)])

    def outgoing(step, part):
        target = lax.rem(place + step, ring)
        return jnp.concatenate(
            [
                lax.dynamic_slice(w, (target, part * part_rows, 0), (1, part_rows, width))
                for w in (gate_weight, up_weight, down_weight)
            ],
            axis=1,
        )

    def over_z(pieces):
        order = sorted(range(1, ring), key=lambda step: abs(2 * step - ring))
        return [shifted(pieces[step], "zhi", step) for step in order] + [pieces[0]]

    def over_plane(part):
        return lax.all_gather(part, ("y", "core"), axis=0, tiled=True)

    def joined(pieces):
        return jnp.concatenate(pieces, axis=0)

    early = tied(*[outgoing(step, 0) for step in range(ring)])
    late = tied(*[outgoing(step, 1) for step in range(ring)])
    first = joined(tied(*over_z(list(early))))
    first, *late = tied(first, *late)
    second = joined(tied(*over_z(late)))
    tokens, second = tied(tokens, second)
    first, second = over_plane(first), over_plane(second)

    flat_ids = expert_ids[:, 0]
    matches = (flat_ids[:, None] == jnp.arange(experts, dtype=jnp.int32)[None, :]).astype(jnp.int32)
    rank_of = jnp.sum((jnp.cumsum(matches, axis=0) - 1) * matches, axis=1)
    position = flat_ids * CAP + rank_of
    selector = (position[None, :] == jnp.arange(slots, dtype=jnp.int32)[:, None]).astype(jnp.bfloat16)
    packed = jnp.dot(selector, tokens, preferred_element_type=jnp.float32).astype(jnp.bfloat16)
    packed = packed.reshape(experts, CAP * CHUNKS, chunk)
    arrived = lax.all_to_all(packed, routes, split_axis=0, concat_axis=0, tiled=True)

    result = swiglu(arrived.reshape(slots, width), [first, second])
    result = result.reshape(experts, CAP * CHUNKS, chunk)
    returned = lax.all_to_all(result, routes, split_axis=0, concat_axis=0, tiled=True)
    returned = returned.reshape(slots, width)
    output = lax.dot_general(
        selector, returned, (((0,), (0,)), ((), ())), preferred_element_type=jnp.float32
    )
    return output.astype(jnp.bfloat16)


def solution(mesh):
    fine = Mesh(mesh.devices.reshape(4, 4, 4, 4, 2), ("x", "zlo", "zhi", "y", "core"))
    everyone = ("x", "zlo", "zhi", "y", "core")
    group = ("x", "zlo")
    sub = ("zhi", "y", "core")
    return jax.shard_map(
        shards,
        mesh=fine,
        in_specs=(
            P(everyone, None),
            P(everyone, None),
            P(group, sub, None),
            P(group, sub, None),
            P(group, sub, None),
        ),
        out_specs=P(everyone, None),
        check_vma=False,
    )
```

```python
import jax
import jax.numpy as jnp
from jax import lax
from jax.experimental import pallas as pl
from jax.experimental.pallas import tpu as pltpu
from jax.sharding import Mesh, PartitionSpec as P

CAP = 3
CHUNKS = 8
STEPS = 4
AHEAD = 2
MIB = 1 << 20


def swiglu_kernel(x_ref, gate_ref, pair_ref, out_ref, gates, pairs, total, arrival):
    blocks, rows, width = gate_ref.shape
    group = blocks // STEPS
    copies = []
    for i in range(STEPS):
        part = pl.ds(i * group, group)
        copies.append(
            (
                pltpu.make_async_copy(gate_ref.at[part], gates.at[part], arrival.at[2 * i]),
                pltpu.make_async_copy(pair_ref.at[part], pairs.at[part], arrival.at[2 * i + 1]),
            )
        )
    for gate_copy, pair_copy in copies[:AHEAD]:
        gate_copy.start()
        pair_copy.start()
    across = (((1,), (1,)), ((), ()))

    def score(matrix):
        return lax.dot_general(x_ref[...], matrix, across, preferred_element_type=jnp.float32)

    for i, (gate_copy, pair_copy) in enumerate(copies):
        part = slice(i * group, (i + 1) * group)
        gate_copy.wait()
        pair_copy.wait()
        for gate_later, pair_later in copies[i + AHEAD : i + AHEAD + 1]:
            gate_later.start()
            pair_later.start()
        gate = score(gates[part].reshape(group * rows, width))
        up = score(pairs[part, :rows, :].reshape(group * rows, width))
        hidden = (gate / (1.0 + jnp.exp(-gate)) * up).astype(jnp.bfloat16)
        down = pairs[part, rows:, :].reshape(group * rows, width)
        product = jnp.dot(hidden, down, preferred_element_type=jnp.float32)
        if i == 0:
            total[...] = product
        elif i < STEPS - 1:
            total[...] += product
        else:
            out_ref[...] = (total[...] + product).astype(out_ref.dtype)


def swiglu(x, gate, pair):
    slots, width = x.shape
    units = gate.shape[0] * gate.shape[1]
    return pl.pallas_call(
        swiglu_kernel,
        out_shape=jax.ShapeDtypeStruct(x.shape, jnp.bfloat16),
        in_specs=[pl.BlockSpec(memory_space=pltpu.VMEM)]
        + [pl.BlockSpec(memory_space=pl.ANY)] * 2,
        out_specs=pl.BlockSpec(memory_space=pltpu.VMEM),
        scratch_shapes=[
            pltpu.VMEM(gate.shape, jnp.bfloat16),
            pltpu.VMEM(pair.shape, jnp.bfloat16),
            pltpu.VMEM((slots, width), jnp.float32),
            pltpu.SemaphoreType.DMA((2 * STEPS,)),
        ],
        compiler_params=pltpu.CompilerParams(vmem_limit_bytes=48 * MIB),
        cost_estimate=pl.CostEstimate(
            flops=6 * slots * units * width,
            bytes_accessed=6 * units * width + 4 * slots * width,
            transcendentals=slots * units,
        ),
    )(x, gate, pair)


def shards(tokens, expert_ids, gate_weight, up_weight, down_weight):
    exp_dev, _, width = gate_weight.shape
    routes = ("x", "zlo", "zhi")
    experts = exp_dev * lax.axis_size("x") * lax.axis_size("zlo")
    chunk = width // CHUNKS
    slots = experts * CAP

    def tied(*values):
        return lax.optimization_barrier(values)

    def over_z(payload):
        return lax.all_to_all(payload, "zhi", split_axis=0, concat_axis=0, tiled=True)

    def over_plane(part):
        return lax.all_gather(part, ("y", "core"), axis=0, tiled=True)

    late = jnp.concatenate([up_weight, down_weight], axis=1)
    first, late = tied(over_z(gate_weight), late)
    second = over_z(late)
    tokens, second = tied(tokens, second)
    first, second = over_plane(first), over_plane(second)

    flat_ids = expert_ids[:, 0]
    matches = (flat_ids[:, None] == jnp.arange(experts, dtype=jnp.int32)[None, :]).astype(jnp.int32)
    rank_of = jnp.sum((jnp.cumsum(matches, axis=0) - 1) * matches, axis=1)
    position = flat_ids * CAP + rank_of
    selector = (position[None, :] == jnp.arange(slots, dtype=jnp.int32)[:, None]).astype(jnp.bfloat16)
    packed = jnp.dot(selector, tokens, preferred_element_type=jnp.float32).astype(jnp.bfloat16)
    packed = packed.reshape(experts, CAP * CHUNKS, chunk)
    arrived = lax.all_to_all(packed, routes, split_axis=0, concat_axis=0, tiled=True)

    result = swiglu(arrived.reshape(slots, width), first, second)
    result = result.reshape(experts, CAP * CHUNKS, chunk)
    returned = lax.all_to_all(result, routes, split_axis=0, concat_axis=0, tiled=True)
    returned = returned.reshape(slots, width)
    output = lax.dot_general(
        selector, returned, (((0,), (0,)), ((), ())), preferred_element_type=jnp.float32
    )
    return output.astype(jnp.bfloat16)


def solution(mesh):
    fine = Mesh(mesh.devices.reshape(4, 4, 4, 4, 2), ("x", "zlo", "zhi", "y", "core"))
    everyone = ("x", "zlo", "zhi", "y", "core")
    group = ("x", "zlo")
    sub = ("zhi", "y", "core")
    return jax.shard_map(
        shards,
        mesh=fine,
        in_specs=(
            P(everyone, None),
            P(everyone, None),
            P(group, sub, None),
            P(group, sub, None),
            P(group, sub, None),
        ),
        out_specs=P(everyone, None),
        check_vma=False,
    )
```

```python
import jax
import jax.numpy as jnp
from jax import lax
from jax.experimental import pallas as pl
from jax.experimental.pallas import tpu as pltpu
from jax.sharding import Mesh, PartitionSpec as P

CAP = 3
CHUNKS = 8
PARTS = 2
PIECES = 4
AHEAD = 2
MIB = 1 << 20


def swiglu_kernel(x_ref, *refs):
    weights, (out_ref, held, total, arrival) = refs[:-4], refs[-4:]
    pieces, blocks, triple, width = held.shape
    rows = triple // 3
    each = pieces // len(weights)
    copies = [
        pltpu.make_async_copy(
            weights[i // each].at[pl.ds(i % each * blocks, blocks)], held.at[i], arrival.at[i]
        )
        for i in range(pieces)
    ]
    for copy in copies[:AHEAD]:
        copy.start()
    across = (((1,), (1,)), ((), ()))
    for i, copy in enumerate(copies):
        copy.wait()
        for later in copies[i + AHEAD : i + AHEAD + 1]:
            later.start()

        def matrix(which):
            return held[i, :, which * rows : (which + 1) * rows, :].reshape(blocks * rows, width)

        gate = lax.dot_general(x_ref[...], matrix(0), across, preferred_element_type=jnp.float32)
        up = lax.dot_general(x_ref[...], matrix(1), across, preferred_element_type=jnp.float32)
        hidden = (gate / (1.0 + jnp.exp(-gate)) * up).astype(jnp.bfloat16)
        product = jnp.dot(hidden, matrix(2), preferred_element_type=jnp.float32)
        if i == 0:
            total[...] = product
        elif i < len(copies) - 1:
            total[...] += product
        else:
            out_ref[...] = (total[...] + product).astype(out_ref.dtype)


def swiglu(x, weights):
    slots, width = x.shape
    blocks, triple, _ = weights[0].shape
    units = len(weights) * blocks * triple // 3
    return pl.pallas_call(
        swiglu_kernel,
        out_shape=jax.ShapeDtypeStruct(x.shape, jnp.bfloat16),
        in_specs=[pl.BlockSpec(memory_space=pltpu.VMEM)]
        + [pl.BlockSpec(memory_space=pl.ANY)] * len(weights),
        out_specs=pl.BlockSpec(memory_space=pltpu.VMEM),
        scratch_shapes=[
            pltpu.VMEM((PIECES, len(weights) * blocks // PIECES, triple, width), jnp.bfloat16),
            pltpu.VMEM((slots, width), jnp.float32),
            pltpu.SemaphoreType.DMA((PIECES,)),
        ],
        compiler_params=pltpu.CompilerParams(vmem_limit_bytes=48 * MIB),
        cost_estimate=pl.CostEstimate(
            flops=6 * slots * units * width,
            bytes_accessed=6 * units * width + 4 * slots * width,
            transcendentals=slots * units,
        ),
    )(x, *weights)


def shards(tokens, expert_ids, gate_weight, up_weight, down_weight):
    exp_dev, unit_rows, width = gate_weight.shape
    routes = ("x", "zlo", "zhi")
    experts = exp_dev * lax.axis_size("x") * lax.axis_size("zlo")
    chunk = width // CHUNKS
    slots = experts * CAP
    ring = lax.axis_size("zhi")
    place = lax.axis_index("zhi")
    part_rows = unit_rows // PARTS

    def tied(*values):
        return lax.optimization_barrier(values)

    def shifted(value, axis, step):
        size = lax.axis_size(axis)
        return lax.ppermute(value, axis, [(i, (i + step) % size) for i in range(size)])

    def outgoing(step, part):
        target = lax.rem(place + step, ring)
        return jnp.concatenate(
            [
                lax.dynamic_slice(w, (target, part * part_rows, 0), (1, part_rows, width))
                for w in (gate_weight, up_weight, down_weight)
            ],
            axis=1,
        )

    def over_z(pieces):
        order = sorted(range(1, ring), key=lambda step: abs(2 * step - ring))
        return [shifted(pieces[step], "zhi", step) for step in order] + [pieces[0]]

    def over_plane(part):
        return lax.all_gather(part, ("y", "core"), axis=0, tiled=True)

    def joined(pieces):
        return jnp.concatenate(pieces, axis=0)

    early = tied(*[outgoing(step, 0) for step in range(ring)])
    late = tied(*[outgoing(step, 1) for step in range(ring)])
    first = joined(tied(*over_z(list(early))))
    first, *late = tied(first, *late)
    second = joined(tied(*over_z(late)))

    flat_ids = expert_ids[:, 0]
    matches = (flat_ids[:, None] == jnp.arange(experts, dtype=jnp.int32)[None, :]).astype(jnp.int32)
    rank_of = jnp.sum((jnp.cumsum(matches, axis=0) - 1) * matches, axis=1)
    position = flat_ids * CAP + rank_of
    selector = (position[None, :] == jnp.arange(slots, dtype=jnp.int32)[:, None]).astype(jnp.bfloat16)
    packed = jnp.dot(selector, tokens, preferred_element_type=jnp.float32).astype(jnp.bfloat16)
    columns = lax.axis_size("x")
    depth = experts // columns
    message = CAP * CHUNKS
    packed = packed.reshape(columns, depth * message, chunk)
    packed = lax.all_to_all(packed, "x", split_axis=0, concat_axis=0, tiled=True)
    packed = packed.reshape(columns, depth, message, chunk).swapaxes(0, 1)
    packed, second = tied(packed.reshape(depth, columns * message, chunk), second)
    first, second = over_plane(first), over_plane(second)
    arrived = lax.all_to_all(packed, ("zlo", "zhi"), split_axis=0, concat_axis=0, tiled=True)
    arrived = arrived.reshape(depth, columns, message, chunk).swapaxes(0, 1)

    result = swiglu(arrived.reshape(slots, width), [first, second])
    result = result.reshape(experts, CAP * CHUNKS, chunk)
    returned = lax.all_to_all(result, routes, split_axis=0, concat_axis=0, tiled=True)
    returned = returned.reshape(slots, width)
    output = lax.dot_general(
        selector, returned, (((0,), (0,)), ((), ())), preferred_element_type=jnp.float32
    )
    return output.astype(jnp.bfloat16)


def solution(mesh):
    fine = Mesh(mesh.devices.reshape(4, 4, 4, 4, 2), ("x", "zlo", "zhi", "y", "core"))
    everyone = ("x", "zlo", "zhi", "y", "core")
    group = ("x", "zlo")
    sub = ("zhi", "y", "core")
    return jax.shard_map(
        shards,
        mesh=fine,
        in_specs=(
            P(everyone, None),
            P(everyone, None),
            P(group, sub, None),
            P(group, sub, None),
            P(group, sub, None),
        ),
        out_specs=P(everyone, None),
        check_vma=False,
    )
```

```python
import jax
import jax.numpy as jnp
from jax import lax
from jax.experimental import pallas as pl
from jax.experimental.pallas import tpu as pltpu
from jax.sharding import Mesh, PartitionSpec as P

CAP = 3
CHUNKS = 8
PARTS = 2
PIECES = 4
AHEAD = 2
MIB = 1 << 20


def swiglu_kernel(x_ref, *refs):
    weights, (out_ref, held, total, arrival) = refs[:-4], refs[-4:]
    pieces, blocks, triple, width = held.shape
    rows = triple // 3
    each = pieces // len(weights)
    copies = [
        pltpu.make_async_copy(
            weights[i // each].at[pl.ds(i % each * blocks, blocks)], held.at[i], arrival.at[i]
        )
        for i in range(pieces)
    ]
    for copy in copies[:AHEAD]:
        copy.start()
    across = (((1,), (1,)), ((), ()))
    for i, copy in enumerate(copies):
        copy.wait()
        for later in copies[i + AHEAD : i + AHEAD + 1]:
            later.start()

        def matrix(which):
            return held[i, :, which * rows : (which + 1) * rows, :].reshape(blocks * rows, width)

        gate = lax.dot_general(x_ref[...], matrix(0), across, preferred_element_type=jnp.float32)
        up = lax.dot_general(x_ref[...], matrix(1), across, preferred_element_type=jnp.float32)
        hidden = (gate / (1.0 + jnp.exp(-gate)) * up).astype(jnp.bfloat16)
        product = jnp.dot(hidden, matrix(2), preferred_element_type=jnp.float32)
        if i == 0:
            total[...] = product
        elif i < len(copies) - 1:
            total[...] += product
        else:
            out_ref[...] = (total[...] + product).astype(out_ref.dtype)


def swiglu(x, weights):
    slots, width = x.shape
    blocks, triple, _ = weights[0].shape
    units = len(weights) * blocks * triple // 3
    return pl.pallas_call(
        swiglu_kernel,
        out_shape=jax.ShapeDtypeStruct(x.shape, jnp.bfloat16),
        in_specs=[pl.BlockSpec(memory_space=pltpu.VMEM)]
        + [pl.BlockSpec(memory_space=pl.ANY)] * len(weights),
        out_specs=pl.BlockSpec(memory_space=pltpu.VMEM),
        scratch_shapes=[
            pltpu.VMEM((PIECES, len(weights) * blocks // PIECES, triple, width), jnp.bfloat16),
            pltpu.VMEM((slots, width), jnp.float32),
            pltpu.SemaphoreType.DMA((PIECES,)),
        ],
        compiler_params=pltpu.CompilerParams(vmem_limit_bytes=48 * MIB),
        cost_estimate=pl.CostEstimate(
            flops=6 * slots * units * width,
            bytes_accessed=6 * units * width + 4 * slots * width,
            transcendentals=slots * units,
        ),
    )(x, *weights)


def shards(tokens, expert_ids, gate_weight, up_weight, down_weight):
    exp_dev, unit_rows, width = gate_weight.shape
    routes = ("x", "zlo", "zhi")
    experts = exp_dev * lax.axis_size("x") * lax.axis_size("zlo")
    chunk = width // CHUNKS
    slots = experts * CAP
    ring = lax.axis_size("zhi")
    place = lax.axis_index("zhi")
    part_rows = unit_rows // PARTS

    def tied(*values):
        return lax.optimization_barrier(values)

    def shifted(value, axis, step):
        size = lax.axis_size(axis)
        return lax.ppermute(value, axis, [(i, (i + step) % size) for i in range(size)])

    def outgoing(step, part):
        target = lax.rem(place + step, ring)
        return jnp.concatenate(
            [
                lax.dynamic_slice(w, (target, part * part_rows, 0), (1, part_rows, width))
                for w in (gate_weight, up_weight, down_weight)
            ],
            axis=1,
        )

    def over_z(pieces):
        order = sorted(range(1, ring), key=lambda step: abs(2 * step - ring))
        return [shifted(pieces[step], "zhi", step) for step in order] + [pieces[0]]

    def over_plane(part):
        return lax.all_gather(part, ("y", "core"), axis=0, tiled=True)

    def joined(pieces):
        return jnp.concatenate(pieces, axis=0)

    flat_ids = expert_ids[:, 0]
    matches = (flat_ids[:, None] == jnp.arange(experts, dtype=jnp.int32)[None, :]).astype(jnp.int32)
    rank_of = jnp.sum((jnp.cumsum(matches, axis=0) - 1) * matches, axis=1)
    position = flat_ids * CAP + rank_of
    selector = (position[None, :] == jnp.arange(slots, dtype=jnp.int32)[:, None]).astype(jnp.bfloat16)
    packed = jnp.dot(selector, tokens, preferred_element_type=jnp.float32).astype(jnp.bfloat16)
    columns = lax.axis_size("x")
    depth = experts // columns
    message = CAP * CHUNKS
    packed = packed.reshape(columns, depth * message, chunk)
    packed = lax.all_to_all(packed, "x", split_axis=0, concat_axis=0, tiled=True)
    packed = packed.reshape(columns, depth, message, chunk).swapaxes(0, 1)
    early = tied(*[outgoing(step, 0) for step in range(ring)])
    late = tied(*[outgoing(step, 1) for step in range(ring)])
    first = joined(tied(*over_z(list(early))))
    first, packed, *late = tied(first, packed, *late)
    second = joined(tied(*over_z(late)))
    packed, second = tied(packed.reshape(depth, columns * message, chunk), second)
    first, second = over_plane(first), over_plane(second)
    arrived = lax.all_to_all(packed, ("zlo", "zhi"), split_axis=0, concat_axis=0, tiled=True)
    arrived = arrived.reshape(depth, columns, message, chunk).swapaxes(0, 1)

    result = swiglu(arrived.reshape(slots, width), [first, second])
    result = result.reshape(experts, CAP * CHUNKS, chunk)
    returned = lax.all_to_all(result, routes, split_axis=0, concat_axis=0, tiled=True)
    returned = returned.reshape(slots, width)
    output = lax.dot_general(
        selector, returned, (((0,), (0,)), ((), ())), preferred_element_type=jnp.float32
    )
    return output.astype(jnp.bfloat16)


def solution(mesh):
    fine = Mesh(mesh.devices.reshape(4, 4, 4, 4, 2), ("x", "zlo", "zhi", "y", "core"))
    everyone = ("x", "zlo", "zhi", "y", "core")
    group = ("x", "zlo")
    sub = ("zhi", "y", "core")
    return jax.shard_map(
        shards,
        mesh=fine,
        in_specs=(
            P(everyone, None),
            P(everyone, None),
            P(group, sub, None),
            P(group, sub, None),
            P(group, sub, None),
        ),
        out_specs=P(everyone, None),
        check_vma=False,
    )
```
